32 devices in a mesh: row: 8 (over z, y), col: 4 (over x, core).
Axes of the slice: x: 2, y: 2, z: 4, core: 2. Of those that a mesh axis runs over, the one named last changes fastest.
Arguments:
- amplitudes: bfloat16 [1024, 32768], P('row', 'col'), may hold values from -6 to 6
- amp_mask: int32 [32, 128], P('row', 'col'), may hold values from 0 to 1, as said below
- integrals: bfloat16 [16384, 32768], P('row', 'col'), may hold values from -0.0625 to 0.0625
- int_mask: int32 [64, 128], P('row', 'col'), may hold values 0 or 1
- occ_energy: float32 [1024], P('col'), may hold values from -1.5 to -0.5
- vir_energy: float32 [16384], P('row'), may hold values from 0.5 to 1.5
Outputs:
- residual: bfloat16 [1024, 16384], P('col', 'row')
The draws below stay inside these ranges and needn't reach their ends.
Inputs may be any that keep to these rules, and one draw needn't show every extreme that they name: In every row of amp_mask, each aligned group of 8 consecutive entries holds exactly 4 ones.
All inputs are finite; a program needn't handle non-finite values. No bound on the sum of `int_mask` on one device may be relied on, other than what follows from the above.
Results may differ from the reference program's by a relative error of at most 0.001.
Values may be sent and summed in bfloat16 or wider, within the bound.
No kernel may reach another device: no remote copies, remote signals or barrier semaphores. Data moves between devices by JAX's collectives and lax.ppermute only.
A program may use at most 192 MiB of HBM per device.

```python
import jax
import jax.numpy as jnp
from jax import lax

TILE = 256
IJ_BLK = 32
GRP = 8
AB = 16384
CD = 32768
IJ = 1024


def draw_amp_mask(key, part):
    nrow = IJ // IJ_BLK
    ngroup = CD // TILE // GRP
    scores = jax.random.randint(jax.random.fold_in(key, 17), (nrow, ngroup, GRP), 0, 2 ** 20)
    distinct = scores * GRP + jnp.arange(GRP, dtype=jnp.int32)[None, None, :]
    order = jnp.argsort(distinct, axis=2)
    ranks = jnp.argsort(order, axis=2)
    return (ranks < GRP // 2).astype(jnp.int32).reshape(nrow, ngroup * GRP)


def set_ends(drawn, stream_key, low, high):
    longest = drawn.shape.index(max(drawn.shape))
    spots = []
    for shift in (0, 1):
        where = [jax.random.randint(jax.random.fold_in(stream_key, axis), (), 0, length) for axis, length in enumerate(drawn.shape)]
        where[longest] = (where[longest] + shift) % drawn.shape[longest]
        spots.append(tuple(where))
    return drawn.at[spots[0]].set(low).at[spots[1]].set(high)


def with_spikes(array, key, source, target, shards_of, factor):
    owner, partner = [(jnp.arange(array.shape[dim]) // (array.shape[dim] // shards_of)).reshape([-1 if axis == dim else 1 for axis in range(array.ndim)]) for dim in (source, target)]
    chosen = jax.random.permutation(key, shards_of)[partner]
    strong = (owner == chosen) | (owner == (partner + shards_of // 2) % shards_of)
    return jnp.where(strong, factor * array, array)


def block_scale(key, shape, shards, smallest, high):
    loudness, own = 1.0, jax.random.fold_in(key, 6)
    for axis_at, blocks in shards:
        heights = jnp.exp(jax.random.uniform(jax.random.fold_in(own, axis_at), (blocks,), jnp.float32, smallest / len(shards), high / len(shards)))
        loudness = loudness * jnp.repeat(heights, shape[axis_at] // blocks).reshape([-1 if axis == axis_at else 1 for axis in range(len(shape))])
    return loudness


def centred(key, dims, deviation, bound, pieces=(), kind=jnp.bfloat16):
    result = deviation * jax.random.normal(key, dims, jnp.float32)
    if pieces:
        result = result * block_scale(key, dims, pieces, -0.22, 0.18)
    return jnp.clip(result, -bound, bound).astype(kind)


def noise_with(key, dims, scale, reach, split, heavy, held_as=jnp.bfloat16):
    result = scale * jax.random.normal(key, dims, jnp.float32)
    if split:
        result = result * block_scale(key, dims, split, -0.22, 0.18)
    return jnp.clip(with_spikes(result, jax.random.fold_in(key, 3), *heavy), -reach, reach).astype(held_as)


def setup_inputs(seed: int = 0) -> dict:
    key_of = jax.random.split(jax.random.key(seed), 7)
    amplitudes = noise_with(key_of[0], (IJ, CD), 1.0, 6.0, ((0, 8), (1, 4)), (1, 0, 8, 2.0))
    amp_mask = draw_amp_mask(jax.random.fold_in(key_of[6], 71), 0)
    integrals = centred(key_of[2], (AB, CD), (CD // 4) ** -0.5, 0.0625, ((0, 8), (1, 4)))
    int_mask = set_ends((jax.random.randint(key_of[3], (AB // TILE, CD // TILE), 0, 2) < 1).astype(jnp.int32), jax.random.fold_in(key_of[3], 1), 0, 1)
    occ_energy = jnp.clip(-1.5 + 1.0 * jax.random.uniform(key_of[4], (IJ,), jnp.float32) ** block_scale(key_of[4], (IJ,), ((0, 4),), -0.2, 0.2), -1.5, -0.5)
    vir_energy = jnp.clip(0.5 + 1.0 * jax.random.uniform(key_of[5], (AB,), jnp.float32) ** block_scale(key_of[5], (AB,), ((0, 8),), -0.2, 0.2), 0.5, 1.5)
    return dict(amplitudes=amplitudes, amp_mask=amp_mask, integrals=integrals, int_mask=int_mask, occ_energy=occ_energy, vir_energy=vir_energy)


def reference(amplitudes, amp_mask, integrals, int_mask, occ_energy, vir_energy):
    amp_keep = jnp.repeat(jnp.repeat(amp_mask, IJ_BLK, axis=0), TILE, axis=1)
    amp_used = jnp.where(amp_keep == 1, amplitudes, jnp.zeros_like(amplitudes))

    def tile_rows(args):
        block, keep = args
        keep_cols = jnp.repeat(keep, TILE)
        used = jnp.where(keep_cols[None, :] == 1, block, jnp.zeros_like(block))
        return jnp.dot(amp_used, used.T, preferred_element_type=jnp.float32)

    blocks = integrals.reshape(AB // TILE, TILE, CD)
    parts = lax.map(tile_rows, (blocks, int_mask))
    ladder = jnp.transpose(parts, (1, 0, 2)).reshape(IJ, AB)
    denom = vir_energy[None, :] - occ_energy[:, None]
    return (ladder / denom).astype(jnp.bfloat16)
```

```python
import functools

import jax
import jax.numpy as jnp
from jax import lax
from jax.experimental import pallas as pl
from jax.experimental.pallas import tpu as pltpu
from jax.sharding import PartitionSpec as P

TILE = 256
IJ_BLK = 32
GRP = 8
KEPT = GRP // 2
LANES = 128
META = 16
PIECE = 2 * IJ_BLK
FLOWS = 4
NBUF = 12
TOP = 32000.0
OCTAVE = 64.0
LN2 = 0.6931471805599453
FLOOR = 1e-30
VMEM = pltpu.VMEM
SMEM = pltpu.SMEM


def vmem():
    return pl.BlockSpec(memory_space=VMEM)


def smem():
    return pl.BlockSpec(memory_space=SMEM)


def pack_kernel(mask_ref, amp_ref, *outs):
    nblock, ntile = mask_ref.shape
    per = nblock // FLOWS
    groups = ntile // GRP
    slots = groups * KEPT
    lane = lax.broadcasted_iota(jnp.int32, (META, LANES), 1)
    for flow in range(FLOWS):
        out = outs[flow]
        meta = jnp.zeros((META, LANES), jnp.int32)
        for q in range(per):
            block = flow * per + q
            rows = slice(block * IJ_BLK, (block + 1) * IJ_BLK)
            for g in range(groups):
                count, bits = jnp.int32(0), jnp.int32(0)
                for j in range(GRP):
                    t = g * GRP + j
                    here = mask_ref[block, t]
                    base = (q * slots + g * KEPT + count) * PIECE

                    @pl.when(here == 1)
                    def _():
                        for half in range(2):
                            at = pl.multiple_of(base + half * IJ_BLK, IJ_BLK)
                            out[pl.ds(at, IJ_BLK), :] = amp_ref[
                                rows,
                                t * TILE + half * LANES : t * TILE + (half + 1) * LANES,
                            ]

                    count += here
                    bits += here << j
                meta = jnp.where(lane == q * groups + g, bits, meta)
        out[per * slots * PIECE :, :] = meta.astype(jnp.float32).astype(jnp.bfloat16)


def pack(amplitudes, amp_mask):
    nblock, ntile = amp_mask.shape
    rows = nblock // FLOWS * (ntile // 2) * PIECE + META
    return pl.pallas_call(
        pack_kernel,
        out_shape=[jax.ShapeDtypeStruct((rows, LANES), jnp.bfloat16)] * FLOWS,
        in_specs=[smem(), vmem()],
        out_specs=[vmem()] * FLOWS,
        compiler_params=pltpu.CompilerParams(vmem_limit_bytes=16 * 2**20),
        name="pack",
    )(amp_mask, amplitudes)


def list_kernel(half_ref, mask_ref, list_ref, off_ref):
    nab, ntile = mask_ref.shape
    first = (1 - half_ref[0]) * (nab // 2)

    def row(ii, count):
        i = lax.rem(ii + first, nab)
        off_ref[ii] = count

        def col(t, count):
            list_ref[count] = i * ntile + t
            return count + mask_ref[i, t]

        return lax.fori_loop(0, ntile, col, count)

    off_ref[nab] = lax.fori_loop(0, nab, row, jnp.int32(0))


def make_list(half, int_mask):
    nab, ntile = int_mask.shape
    return pl.pallas_call(
        list_kernel,
        out_shape=[
            jax.ShapeDtypeStruct((nab * ntile + 1,), jnp.int32),
            jax.ShapeDtypeStruct((nab + 1,), jnp.int32),
        ],
        in_specs=[smem(), smem()],
        out_specs=[smem(), smem()],
        name="tile_list",
    )(half, int_mask)


def ladder_kernel(
    nchunk, per, ntile, list_ref, off_ref, int_ref, *rest
):
    chunks, (other_ref, mine_ref), scratch = (
        rest[:nchunk],
        rest[nchunk : nchunk + 2],
        rest[nchunk + 2 :],
    )
    dense, bufs, meta_v, meta_s, sems, meta_sem = scratch
    nab = off_ref.shape[0] - 1
    groups = ntile // GRP
    slots = groups * KEPT
    total = off_ref[nab]

    def fetch(n):
        at = list_ref[n]
        i, t = at // ntile, lax.rem(at, ntile)
        slot = lax.rem(n, NBUF)
        return pltpu.make_async_copy(
            int_ref.at[
                pl.ds(pl.multiple_of(i * TILE, TILE), TILE),
                pl.ds(pl.multiple_of(t * TILE, TILE), TILE),
            ],
            bufs.at[slot],
            sems.at[slot],
        )

    for n in range(NBUF):

        @pl.when(n < total)
        def _():
            fetch(n).start()

    for c in range(nchunk):
        head = chunks[c][per * slots * PIECE :, :].astype(jnp.float32)
        meta_v[c * 8 : (c + 1) * 8, :] = head[:8].astype(jnp.int32)
    copy = pltpu.make_async_copy(meta_v, meta_s, meta_sem)
    copy.start()
    copy.wait()
    zero = jnp.zeros((IJ_BLK, LANES), jnp.bfloat16)
    for c in range(nchunk):
        for q in range(per):
            row = (c * per + q) * IJ_BLK
            for g in range(groups):
                bits = meta_s[c * 8, q * groups + g]
                count = jnp.int32(0)
                for j in range(GRP):
                    here = (bits >> j) & 1
                    base = (
                        q * slots + g * KEPT + jnp.minimum(count, KEPT - 1)
                    ) * PIECE
                    for half in range(2):
                        at = pl.multiple_of(base + half * IJ_BLK, IJ_BLK)
                        tile = chunks[c][pl.ds(at, IJ_BLK), :]
                        dense[
                            g * GRP + j,
                            row : row + IJ_BLK,
                            half * LANES : (half + 1) * LANES,
                        ] = jnp.where(here == 1, tile, zero)
                    count += here

    for ii in range(nab):
        out = other_ref if ii < nab // 2 else mine_ref
        cols = slice((ii % (nab // 2)) * TILE, (ii % (nab // 2) + 1) * TILE)
        out[:, cols] = jnp.zeros((out.shape[0], TILE), jnp.float32)

        def step(n, carry):
            slot = lax.rem(n, NBUF)
            t = lax.rem(list_ref[n], ntile)
            fetch(n).wait()
            out[:, cols] += lax.dot_general(
                dense[t],
                bufs[slot],
                (((1,), (1,)), ((), ())),
                preferred_element_type=jnp.float32,
            )

            @pl.when(n + NBUF < total)
            def _():
                fetch(n + NBUF).start()

            return carry

        lax.fori_loop(off_ref[ii], off_ref[ii + 1], step, 0)


def ladder(chunks, tile_list, offsets, integrals):
    nchunk = len(chunks)
    rows_ab, rows_cd = integrals.shape
    ntile = rows_cd // TILE
    per = (chunks[0].shape[0] - META) // (ntile // 2 * PIECE)
    m = nchunk * per * IJ_BLK
    out = jax.ShapeDtypeStruct((m, rows_ab // 2), jnp.float32)
    return pl.pallas_call(
        functools.partial(ladder_kernel, nchunk, per, ntile),
        out_shape=[out, out],
        in_specs=[smem(), smem(), pl.BlockSpec(memory_space=pl.ANY)]
        + [vmem()] * nchunk,
        out_specs=[vmem(), vmem()],
        scratch_shapes=[
            VMEM((ntile, m, TILE), jnp.bfloat16),
            VMEM((NBUF, TILE, TILE), jnp.bfloat16),
            VMEM((nchunk * 8, LANES), jnp.int32),
            SMEM((nchunk * 8, LANES), jnp.int32),
            pltpu.SemaphoreType.DMA((NBUF,)),
            pltpu.SemaphoreType.DMA,
        ],
        compiler_params=pltpu.CompilerParams(vmem_limit_bytes=24 * 2**20),
        cost_estimate=pl.CostEstimate(
            flops=m * rows_ab * rows_cd,
            bytes_accessed=rows_ab * rows_cd,
            transcendentals=0,
        ),
        name="ladder",
    )(tile_list, offsets, integrals, *chunks)


def code_kernel(mine_ref, got_ref, sum_ref, code_ref):
    rows, width = mine_ref.shape

    def step(b, carry):
        at = pl.ds(pl.multiple_of(b * IJ_BLK, IJ_BLK), IJ_BLK)
        total = mine_ref[at, :] + got_ref[at, :]
        sum_ref[at, :] = total
        peak = jnp.max(jnp.abs(total), axis=1, keepdims=True)
        level = jnp.ceil(jnp.log(jnp.maximum(peak, FLOOR)) * (OCTAVE / LN2))
        up = jnp.exp(level * (-LN2 / OCTAVE)) * TOP
        code_ref[at, :width] = (
            jnp.round(total * up).astype(jnp.int32).astype(jnp.int16)
        )
        code_ref[at, width:] = jnp.broadcast_to(
            level.astype(jnp.int32), (IJ_BLK, LANES)
        ).astype(jnp.int16)
        return carry

    lax.fori_loop(0, rows // IJ_BLK, step, 0)


def code(mine, got):
    rows, width = mine.shape
    return pl.pallas_call(
        code_kernel,
        out_shape=[
            jax.ShapeDtypeStruct((rows, width), jnp.float32),
            jax.ShapeDtypeStruct((rows, width + LANES), jnp.int16),
        ],
        in_specs=[vmem()] * 2,
        out_specs=[vmem()] * 2,
        compiler_params=pltpu.CompilerParams(vmem_limit_bytes=16 * 2**20),
        name="code",
    )(mine, got)


def final_kernel(
    nsum, npeer, blocks, n, ncol, src_ref, place_ref, occ_ref, vir_ref, *rest
):
    sums, codes, out = (
        rest[:nsum],
        [
            rest[nsum + j * npeer : nsum + (j + 1) * npeer]
            for j in range(nsum)
        ],
        rest[nsum * (1 + npeer)],
    )
    width = vir_ref.shape[1]
    chip, half = place_ref[0], place_ref[1]
    rows_out = out.shape[1]
    vir = vir_ref[...]
    for j, batch in enumerate(blocks):
        for b, (which, block) in enumerate(batch):
            src = src_ref[which]
            owner = src * ncol // n
            row = lax.rem(src, n // ncol) * (rows_out * ncol // n) + block * IJ_BLK
            at = slice(b * IJ_BLK, (b + 1) * IJ_BLK)

            @pl.when(owner // 2 == chip)
            def _():
                side = lax.rem(owner + half, 2)
                to = pl.multiple_of(row, IJ_BLK)
                total = sums[j][at, :]
                for got in codes[j]:
                    level = got[at, width:].astype(jnp.int32).astype(jnp.float32)
                    down = jnp.exp(level[:, :1] * (LN2 / OCTAVE)) * (1.0 / TOP)
                    coded = got[at, :width].astype(jnp.int32).astype(jnp.float32)
                    total = total + coded * down
                denom = vir - occ_ref[side, pl.ds(to, IJ_BLK), :]
                out[side, pl.ds(to, IJ_BLK), :] = (total / denom).astype(out.dtype)


def final(sums, codes, blocks, n, ncol, src, place, occ, vir):
    npeer = len(codes[0])
    flat = [c for batch in codes for c in batch]
    width = vir.shape[1]
    return pl.pallas_call(
        functools.partial(final_kernel, len(sums), npeer, blocks, n, ncol),
        out_shape=jax.ShapeDtypeStruct((2, occ.shape[1], width), jnp.bfloat16),
        in_specs=[smem(), smem()] + [vmem()] * (2 + len(sums) + len(flat)),
        out_specs=vmem(),
        compiler_params=pltpu.CompilerParams(vmem_limit_bytes=32 * 2**20),
        name="final",
    )(src, place, occ, vir, *sums, *flat)


def body(n, ncol, amplitudes, amp_mask, integrals, int_mask, occ_energy, vir_energy):
    cycle = list(range(0, n, 2)) + list(range(n - 1, 0, -2))
    ahead = [(cycle[p], cycle[(p + 1) % n]) for p in range(n)]
    behind = [(b, a) for a, b in ahead]
    row, col = lax.axis_index("row"), lax.axis_index("col")
    half = lax.rem(col, 2)
    core = [(c, c ^ 1) for c in range(ncol)]
    nblock = amp_mask.shape[0]
    per = nblock // FLOWS
    table = [None] * n
    for p in range(n):
        table[cycle[p]] = [cycle[p]] + [
            cycle[(p + sign * s) % n] for s in range(1, n) for sign in (-1, 1)
        ]
    src = jnp.array(table, jnp.int32)[row]
    place = jnp.stack([col // 2, half]).astype(jnp.int32)
    width = integrals.shape[0] // 2

    flows = pack(amplitudes, amp_mask)
    tile_list, offsets = make_list(half.reshape(1).astype(jnp.int32), int_mask)
    occ_other = lax.ppermute(occ_energy, "col", core)
    occ = jnp.stack([occ_energy, occ_other])[:, :, None]
    vir = lax.dynamic_slice_in_dim(vir_energy, half * width, width)[None, :]

    parts = [[(flows[f], 0, f * per) for f in range(FLOWS)]]
    held = list(flows)
    for s in range(1, n):
        held = [
            lax.ppermute(h, "row", ahead if f < FLOWS // 2 else behind)
            for f, h in enumerate(held)
        ]
        parts.append(
            [
                (h, 2 * s - 1 + (f >= FLOWS // 2), f * per)
                for f, h in enumerate(held)
            ]
        )
    batches, now = [], []
    for s in range(n):
        now += parts[s]
        if s % 2 == 1 and s < n - 2 or s >= n - 2:
            batches.append(now)
            now = []
    sums, codes, blocks = [], [], []
    for batch in batches:
        other, mine = ladder([c for c, _, _ in batch], tile_list, offsets, integrals)
        got = lax.ppermute(other, "col", core)
        total, coded = code(mine, got)
        sums.append(total)
        codes.append(
            [
                lax.ppermute(coded, "col", [(c, c ^ (2 * d)) for c in range(ncol)])
                for d in range(1, ncol // 2)
            ]
        )
        blocks.append(
            [(which, b + q) for _, which, b in batch for q in range(per)]
        )
    done = final(sums, codes, blocks, n, ncol, src, place, occ, vir)
    mine, theirs = done[0], done[1]
    got = lax.ppermute(theirs, "col", core)
    return jnp.where(
        half == 0,
        jnp.concatenate([mine, got], axis=1),
        jnp.concatenate([got, mine], axis=1),
    )


def solution(mesh):
    return jax.shard_map(
        functools.partial(body, mesh.shape["row"], mesh.shape["col"]),
        mesh=mesh,
        in_specs=(
            P("row", "col"),
            P("row", "col"),
            P("row", "col"),
            P("row", "col"),
            P("col"),
            P("row"),
        ),
        out_specs=P("col", "row"),
        check_vma=False,
    )
```

```python
import functools

import jax
import jax.numpy as jnp
from jax import lax
from jax.experimental import pallas as pl
from jax.experimental.pallas import tpu as pltpu
from jax.sharding import PartitionSpec as P

TILE = 256
IJ_BLK = 32
GRP = 8
KEPT = GRP // 2
LANES = 128
META = 16
PIECE = 2 * IJ_BLK
FLOWS = 2
RUN = 4
PAR = 4
SLOTS = 4
TOP = 32000.0
OCTAVE = 64.0
LN2 = 0.6931471805599453
FLOOR = 1e-30
VMEM = pltpu.VMEM
SMEM = pltpu.SMEM


def vmem():
    return pl.BlockSpec(memory_space=VMEM)


def smem():
    return pl.BlockSpec(memory_space=SMEM)


def pack_kernel(mask_ref, amp_ref, *rest):
    outs, (held, sems) = rest[:FLOWS], rest[FLOWS:]
    nblock, ntile = mask_ref.shape
    per = nblock // FLOWS
    groups = ntile // GRP
    slots = groups * KEPT
    lane = lax.broadcasted_iota(jnp.int32, (META, LANES), 1)

    def fetch(block):
        rows = pl.ds(block * IJ_BLK, IJ_BLK)
        return pltpu.make_async_copy(amp_ref.at[rows], held.at[rows], sems.at[block])

    order = [flow * per + q for q in range(per) for flow in range(FLOWS)]
    metas = [jnp.zeros((META, LANES), jnp.int32)] * FLOWS
    for block in order:
        fetch(block).start()
    for block in order:
        flow, q = block // per, block % per
        out = outs[flow]
        rows = slice(block * IJ_BLK, (block + 1) * IJ_BLK)
        fetch(block).wait()
        for g in range(groups):
            count, bits = jnp.int32(0), jnp.int32(0)
            for j in range(GRP):
                t = g * GRP + j
                here = mask_ref[block, t]
                base = (q * slots + g * KEPT + count) * PIECE

                @pl.when(here == 1)
                def _():
                    for half in range(2):
                        at = pl.multiple_of(base + half * IJ_BLK, IJ_BLK)
                        out[pl.ds(at, IJ_BLK), :] = held[
                            rows,
                            t * TILE + half * LANES : t * TILE + (half + 1) * LANES,
                        ]

                count += here
                bits += here << j
            metas[flow] = jnp.where(lane == q * groups + g, bits, metas[flow])
    for flow in range(FLOWS):
        meta = metas[flow].astype(jnp.float32).astype(jnp.bfloat16)
        outs[flow][per * slots * PIECE :, :] = meta


def pack(amplitudes, amp_mask):
    nblock, ntile = amp_mask.shape
    rows = nblock // FLOWS * (ntile // 2) * PIECE + META
    return pl.pallas_call(
        pack_kernel,
        out_shape=[jax.ShapeDtypeStruct((rows, LANES), jnp.bfloat16)] * FLOWS,
        in_specs=[smem(), pl.BlockSpec(memory_space=pl.ANY)],
        out_specs=[vmem()] * FLOWS,
        scratch_shapes=[
            VMEM(amplitudes.shape, jnp.bfloat16),
            pltpu.SemaphoreType.DMA((nblock,)),
        ],
        compiler_params=pltpu.CompilerParams(vmem_limit_bytes=60 * 2**20),
        name="pack",
    )(amp_mask, amplitudes)


def list_kernel(half_ref, mask_ref, list_ref):
    nab, ntile = mask_ref.shape
    steps, size, rows_at, steps_at = list_sizes(nab, ntile)
    first = (1 - half_ref[0]) * (nab // 2)
    none = jnp.int32(ntile)

    def clear(k, carry):
        for u in range(GRP):
            list_ref[k * GRP + u] = none
        return carry

    lax.fori_loop(0, rows_at // GRP, clear, 0)
    for k in range(rows_at, steps_at):
        list_ref[k] = jnp.int32(0)

    def row(ii, base):
        i = lax.rem(ii + first, nab)
        at = base * RUN
        for t in range(ntile):
            here = mask_ref[i, t]
            list_ref[at] = jnp.where(here == 1, i * (ntile + 1) + t, none)
            at += here
        runs = (at - base * RUN + RUN - 1) // RUN

        def note(k, carry):
            list_ref[rows_at + base + k] = lax.rem(ii, nab // 2)
            return carry

        lax.fori_loop(0, runs, note, 0)
        return base + runs

    list_ref[steps_at] = jnp.int32(0)
    middle = lax.fori_loop(0, nab // 2, row, jnp.int32(0))
    middle = (middle + PAR - 1) // PAR
    list_ref[steps_at + 1] = middle
    end = lax.fori_loop(nab // 2, nab, row, middle * PAR)
    list_ref[steps_at + 2] = (end + PAR - 1) // PAR


def list_sizes(nab, ntile):
    runs = nab * ((ntile + RUN - 1) // RUN) + 2 * PAR
    rows_at = -(-(runs * RUN + 1) // GRP) * GRP
    return runs // PAR, rows_at + runs + 3, rows_at, rows_at + runs


def make_list(half, int_mask):
    nab, ntile = int_mask.shape
    return pl.pallas_call(
        list_kernel,
        out_shape=jax.ShapeDtypeStruct((list_sizes(nab, ntile)[1],), jnp.int32),
        in_specs=[smem(), smem()],
        out_specs=smem(),
        name="tile_list",
    )(half, int_mask)


def ladder_kernel(nchunk, per, nab, ntile, list_ref, int_ref, *rest):
    chunks, (other_ref, mine_ref), scratch = (
        rest[:nchunk],
        rest[nchunk : nchunk + 2],
        rest[nchunk + 2 :],
    )
    dense, bufs, meta_v, meta_s, sems, meta_sem = scratch
    group = RUN * PAR
    _, _, rows_at, steps_at = list_sizes(nab, ntile)
    groups = ntile // GRP
    slots = groups * KEPT
    total = list_ref[steps_at + 2]

    def start(n):
        slot = lax.rem(n, SLOTS)
        for u in range(group):
            at = list_ref[n * group + u]
            i, t = at // (ntile + 1), lax.rem(at, ntile + 1)
            t = jnp.minimum(t, ntile - 1)
            pltpu.make_async_copy(
                int_ref.at[
                    pl.ds(pl.multiple_of(i * TILE, TILE), TILE),
                    pl.ds(pl.multiple_of(t * TILE, TILE), TILE),
                ],
                bufs.at[slot, u],
                sems.at[slot],
            ).start()

    for n in range(SLOTS):

        @pl.when(n < total)
        def _():
            start(n)

    for c in range(nchunk):
        head = chunks[c][per * slots * PIECE :, :].astype(jnp.float32)
        meta_v[c * 8 : (c + 1) * 8, :] = head[:8].astype(jnp.int32)
    copy = pltpu.make_async_copy(meta_v, meta_s, meta_sem)
    copy.start()
    other_ref[...] = jnp.zeros_like(other_ref)
    mine_ref[...] = jnp.zeros_like(mine_ref)
    dense[ntile] = jnp.zeros(dense.shape[1:], jnp.bfloat16)
    copy.wait()
    zero = jnp.zeros((IJ_BLK, LANES), jnp.bfloat16)
    for c in range(nchunk):
        for q in range(per):
            row = (c * per + q) * IJ_BLK
            for g in range(groups):
                bits = meta_s[c * 8, q * groups + g]
                count = jnp.int32(0)
                for j in range(GRP):
                    here = (bits >> j) & 1
                    base = (
                        q * slots + g * KEPT + jnp.minimum(count, KEPT - 1)
                    ) * PIECE
                    for half in range(2):
                        at = pl.multiple_of(base + half * IJ_BLK, IJ_BLK)
                        tile = chunks[c][pl.ds(at, IJ_BLK), :]
                        dense[
                            g * GRP + j,
                            row : row + IJ_BLK,
                            half * LANES : (half + 1) * LANES,
                        ] = jnp.where(here == 1, tile, zero)
                    count += here

    for side, out in enumerate((other_ref, mine_ref)):

        def step(n, carry):
            slot = lax.rem(n, SLOTS)
            pltpu.make_async_copy(bufs.at[slot], bufs.at[slot], sems.at[slot]).wait()
            parts = []
            for r in range(PAR):
                acc = None
                for u in range(r * RUN, (r + 1) * RUN):
                    t = lax.rem(list_ref[n * group + u], ntile + 1)
                    part = lax.dot_general(
                        dense[t],
                        bufs[slot, u],
                        (((1,), (1,)), ((), ())),
                        preferred_element_type=jnp.float32,
                    )
                    acc = part if acc is None else acc + part
                parts.append(acc)
            for r in range(PAR):
                left = pl.multiple_of(list_ref[rows_at + n * PAR + r] * TILE, TILE)
                out[:, pl.ds(left, TILE)] += parts[r]

            @pl.when(n + SLOTS < total)
            def _():
                start(n + SLOTS)

            return carry

        lax.fori_loop(list_ref[steps_at + side], list_ref[steps_at + side + 1], step, 0)


def ladder(chunks, tile_list, integrals):
    nchunk = len(chunks)
    rows_ab, rows_cd = integrals.shape
    ntile = rows_cd // TILE
    per = (chunks[0].shape[0] - META) // (ntile // 2 * PIECE)
    m = nchunk * per * IJ_BLK
    out = jax.ShapeDtypeStruct((m, rows_ab // 2), jnp.float32)
    return pl.pallas_call(
        functools.partial(ladder_kernel, nchunk, per, rows_ab // TILE, ntile),
        out_shape=[out, out],
        in_specs=[smem(), pl.BlockSpec(memory_space=pl.ANY)]
        + [vmem()] * nchunk,
        out_specs=[vmem(), vmem()],
        scratch_shapes=[
            VMEM((ntile + 1, m, TILE), jnp.bfloat16),
            VMEM((SLOTS, RUN * PAR, TILE, TILE), jnp.bfloat16),
            VMEM((nchunk * 8, LANES), jnp.int32),
            SMEM((nchunk * 8, LANES), jnp.int32),
            pltpu.SemaphoreType.DMA((SLOTS,)),
            pltpu.SemaphoreType.DMA,
        ],
        compiler_params=pltpu.CompilerParams(vmem_limit_bytes=24 * 2**20),
        cost_estimate=pl.CostEstimate(
            flops=2 * m * rows_ab * rows_cd,
            bytes_accessed=rows_ab * rows_cd,
            transcendentals=0,
        ),
        name="ladder",
    )(tile_list, integrals, *chunks)


def code_kernel(mine_ref, got_ref, sum_ref, code_ref):
    rows, width = mine_ref.shape

    def step(b, carry):
        at = pl.ds(pl.multiple_of(b * IJ_BLK, IJ_BLK), IJ_BLK)
        total = mine_ref[at, :] + got_ref[at, :]
        sum_ref[at, :] = total
        peak = jnp.max(jnp.abs(total), axis=1, keepdims=True)
        level = jnp.ceil(jnp.log(jnp.maximum(peak, FLOOR)) * (OCTAVE / LN2))
        up = jnp.exp(level * (-LN2 / OCTAVE)) * TOP
        code_ref[at, :width] = (
            jnp.round(total * up).astype(jnp.int32).astype(jnp.int16)
        )
        code_ref[at, width:] = jnp.broadcast_to(
            level.astype(jnp.int32), (IJ_BLK, LANES)
        ).astype(jnp.int16)
        return carry

    lax.fori_loop(0, rows // IJ_BLK, step, 0)


def code(mine, got):
    rows, width = mine.shape
    return pl.pallas_call(
        code_kernel,
        out_shape=[
            jax.ShapeDtypeStruct((rows, width), jnp.float32),
            jax.ShapeDtypeStruct((rows, width + LANES), jnp.int16),
        ],
        in_specs=[vmem()] * 2,
        out_specs=[vmem()] * 2,
        compiler_params=pltpu.CompilerParams(vmem_limit_bytes=16 * 2**20),
        name="code",
    )(mine, got)


def final_kernel(
    nsum, npeer, blocks, n, ncol, src_ref, place_ref, occ_ref, vir_ref, *rest
):
    sums, codes, out = (
        rest[:nsum],
        [
            rest[nsum + j * npeer : nsum + (j + 1) * npeer]
            for j in range(nsum)
        ],
        rest[-1],
    )
    width = vir_ref.shape[1]
    chip, half = place_ref[0], place_ref[1]
    rows_out = out.shape[1]
    vir = vir_ref[...]
    for j, batch in enumerate(blocks):
        for b, (which, block) in enumerate(batch):
            src = src_ref[which]
            owner = src * ncol // n
            row = lax.rem(src, n // ncol) * (rows_out * ncol // n) + block * IJ_BLK
            at = slice(b * IJ_BLK, (b + 1) * IJ_BLK)

            @pl.when(owner // 2 == chip)
            def _():
                side = lax.rem(owner + half, 2)
                to = pl.multiple_of(row, IJ_BLK)
                total = sums[j][at, :]
                for got in codes[j]:
                    level = got[at, width:].astype(jnp.int32).astype(jnp.float32)
                    down = jnp.exp(level[:, :1] * (LN2 / OCTAVE)) * (1.0 / TOP)
                    coded = got[at, :width].astype(jnp.int32).astype(jnp.float32)
                    total = total + coded * down
                denom = vir - occ_ref[side, pl.ds(to, IJ_BLK), :]
                out[side, pl.ds(to, IJ_BLK), :] = (total / denom).astype(out.dtype)


def final(sums, codes, blocks, n, ncol, src, place, occ, vir, so_far):
    npeer = len(codes[0])
    flat = [c for batch in codes for c in batch]
    width = vir.shape[1]
    more = [] if so_far is None else [so_far]
    return pl.pallas_call(
        functools.partial(final_kernel, len(sums), npeer, blocks, n, ncol),
        out_shape=jax.ShapeDtypeStruct((2, occ.shape[1], width), jnp.bfloat16),
        in_specs=[smem(), smem()] + [vmem()] * (2 + len(sums) + len(flat) + len(more)),
        out_specs=vmem(),
        input_output_aliases={4 + len(sums) + len(flat): 0} if more else {},
        compiler_params=pltpu.CompilerParams(vmem_limit_bytes=32 * 2**20),
        name="final",
    )(src, place, occ, vir, *sums, *flat, *more)


def body(n, ncol, amplitudes, amp_mask, integrals, int_mask, occ_energy, vir_energy):
    cycle = list(range(0, n, 2)) + list(range(n - 1, 0, -2))
    ahead = [(cycle[p], cycle[(p + 1) % n]) for p in range(n)]
    behind = [(b, a) for a, b in ahead]
    row, col = lax.axis_index("row"), lax.axis_index("col")
    half = lax.rem(col, 2)
    core = [(c, c ^ 1) for c in range(ncol)]
    nblock = amp_mask.shape[0]
    per = nblock // FLOWS
    table = [None] * n
    for p in range(n):
        table[cycle[p]] = [cycle[p]] + [
            cycle[(p + sign * s) % n] for s in range(1, n) for sign in (-1, 1)
        ]
    src = jnp.array(table, jnp.int32)[row]
    place = jnp.stack([col // 2, half]).astype(jnp.int32)
    width = integrals.shape[0] // 2

    flows = pack(amplitudes, amp_mask)
    tile_list = make_list(half.reshape(1).astype(jnp.int32), int_mask)
    occ_other = lax.ppermute(occ_energy, "col", core)
    occ = jnp.stack([occ_energy, occ_other])[:, :, None]
    vir = lax.dynamic_slice_in_dim(vir_energy, half * width, width)[None, :]

    def tie(arrays, others):
        return lax.optimization_barrier((arrays, others))

    def ladder_of(steps, coded):
        batch = [part for s in steps for part in parts[s]]
        other, mine = ladder([c for c, _, _ in batch], tile_list, integrals)
        if coded:
            total, peers, blocks = coded.pop()
            other, peers = tie(other, peers)
            coded.append((total, peers, blocks))
        blocks = [(which, b + q) for _, which, b in batch for q in range(per)]
        return lax.ppermute(other, "col", core), mine, blocks

    def code_of(got, mine, blocks):
        total, coded = code(mine, got)
        peers = [
            lax.ppermute(coded, "col", [(c, c ^ (2 * d)) for c in range(ncol)])
            for d in range(1, ncol // 2)
        ]
        return total, peers, blocks

    def final_of(coded, so_far):
        sums, codes, blocks = zip(*coded, strict=True)
        return final(sums, codes, blocks, n, ncol, src, place, occ, vir, so_far)

    parts = [[(flows[f], 0, f * per) for f in range(FLOWS)]]
    held = list(flows)
    waiting, coded = None, []
    for s in range(1, n):
        sent = [
            lax.ppermute(h, "row", ahead if f < FLOWS // 2 else behind)
            for f, h in enumerate(held)
        ]
        if s == 1:
            fixed = [tile_list, occ, vir, src, place]
            held, (tile_list, occ, vir, src, place) = tie(sent, fixed)
        elif s % 2 == 0:
            waiting = ladder_of([s - 2, s - 1], coded)
            held, mine = tie(sent, waiting[1])
            waiting = (waiting[0], mine, waiting[2])
        else:
            total, peers, blocks = code_of(*waiting)
            held, total = tie(sent, total)
            coded.append((total, peers, blocks))
        parts.append(
            [
                (h, 2 * s - 1 + (f >= FLOWS // 2), f * per)
                for f, h in enumerate(held)
            ]
        )
    last = code_of(*ladder_of([n - 2, n - 1], coded))
    done = final_of([last], final_of(coded, None))
    mine, theirs = done[0], done[1]
    got = lax.ppermute(theirs, "col", core)
    return jnp.where(
        half == 0,
        jnp.concatenate([mine, got], axis=1),
        jnp.concatenate([got, mine], axis=1),
    )


def solution(mesh):
    return jax.shard_map(
        functools.partial(body, mesh.shape["row"], mesh.shape["col"]),
        mesh=mesh,
        in_specs=(
            P("row", "col"),
            P("row", "col"),
            P("row", "col"),
            P("row", "col"),
            P("col"),
            P("row"),
        ),
        out_specs=P("col", "row"),
        check_vma=False,
    )
```

```python
import functools

import jax
import jax.numpy as jnp
from jax import lax
from jax.experimental import pallas as pl
from jax.experimental.pallas import tpu as pltpu
from jax.sharding import PartitionSpec as P

TILE = 256
IJ_BLK = 32
GRP = 8
KEPT = GRP // 2
LANES = 128
META = 16
PIECE = 2 * IJ_BLK
FLOWS = 2
RUN = 4
PAR = 4
SLOTS = 4
TOP = 32000.0
OCTAVE = 64.0
LN2 = 0.6931471805599453
FLOOR = 1e-30
VMEM = pltpu.VMEM
SMEM = pltpu.SMEM


def vmem():
    return pl.BlockSpec(memory_space=VMEM)


def smem():
    return pl.BlockSpec(memory_space=SMEM)


def pack_kernel(mask_ref, amp_ref, *rest):
    outs, (held, sems) = rest[:FLOWS], rest[FLOWS:]
    nblock, ntile = mask_ref.shape
    per = nblock // FLOWS
    groups = ntile // GRP
    slots = groups * KEPT
    lane = lax.broadcasted_iota(jnp.int32, (META, LANES), 1)

    def fetch(block):
        rows = pl.ds(block * IJ_BLK, IJ_BLK)
        return pltpu.make_async_copy(amp_ref.at[rows], held.at[rows], sems.at[block])

    order = [flow * per + q for q in range(per) for flow in range(FLOWS)]
    metas = [jnp.zeros((META, LANES), jnp.int32)] * FLOWS
    for block in order:
        fetch(block).start()
    for block in order:
        flow, q = block // per, block % per
        out = outs[flow]
        rows = slice(block * IJ_BLK, (block + 1) * IJ_BLK)
        fetch(block).wait()
        for g in range(groups):
            count, bits = jnp.int32(0), jnp.int32(0)
            for j in range(GRP):
                t = g * GRP + j
                here = mask_ref[block, t]
                base = (q * slots + g * KEPT + count) * PIECE

                @pl.when(here == 1)
                def _():
                    for half in range(2):
                        at = pl.multiple_of(base + half * IJ_BLK, IJ_BLK)
                        out[pl.ds(at, IJ_BLK), :] = held[
                            rows,
                            t * TILE + half * LANES : t * TILE + (half + 1) * LANES,
                        ]

                count += here
                bits += here << j
            metas[flow] = jnp.where(lane == q * groups + g, bits, metas[flow])
    for flow in range(FLOWS):
        meta = metas[flow].astype(jnp.float32).astype(jnp.bfloat16)
        outs[flow][per * slots * PIECE :, :] = meta


def pack(amplitudes, amp_mask):
    nblock, ntile = amp_mask.shape
    rows = nblock // FLOWS * (ntile // 2) * PIECE + META
    return pl.pallas_call(
        pack_kernel,
        out_shape=[jax.ShapeDtypeStruct((rows, LANES), jnp.bfloat16)] * FLOWS,
        in_specs=[smem(), pl.BlockSpec(memory_space=pl.ANY)],
        out_specs=[vmem()] * FLOWS,
        scratch_shapes=[
            VMEM(amplitudes.shape, jnp.bfloat16),
            pltpu.SemaphoreType.DMA((nblock,)),
        ],
        compiler_params=pltpu.CompilerParams(vmem_limit_bytes=16 * 2**20),
        name="pack",
    )(amp_mask, amplitudes)


def list_kernel(half_ref, mask_ref, list_ref):
    nab, ntile = mask_ref.shape
    steps, size, rows_at, steps_at = list_sizes(nab, ntile)
    first = (1 - half_ref[0]) * (nab // 2)
    none = jnp.int32(ntile)

    def clear(k, carry):
        for u in range(GRP):
            list_ref[k * GRP + u] = none
        return carry

    lax.fori_loop(0, rows_at // GRP, clear, 0)
    for k in range(rows_at, steps_at):
        list_ref[k] = jnp.int32(0)

    def row(ii, base):
        i = lax.rem(ii + first, nab)
        at = base * RUN
        for t in range(ntile):
            here = mask_ref[i, t]
            list_ref[at] = jnp.where(here == 1, i * (ntile + 1) + t, none)
            at += here
        runs = (at - base * RUN + RUN - 1) // RUN

        def note(k, carry):
            list_ref[rows_at + base + k] = lax.rem(ii, nab // 2)
            return carry

        lax.fori_loop(0, runs, note, 0)
        return base + runs

    list_ref[steps_at] = jnp.int32(0)
    middle = lax.fori_loop(0, nab // 2, row, jnp.int32(0))
    middle = (middle + PAR - 1) // PAR
    list_ref[steps_at + 1] = middle
    end = lax.fori_loop(nab // 2, nab, row, middle * PAR)
    list_ref[steps_at + 2] = (end + PAR - 1) // PAR


def list_sizes(nab, ntile):
    runs = nab * ((ntile + RUN - 1) // RUN) + 2 * PAR
    rows_at = -(-(runs * RUN + 1) // GRP) * GRP
    return runs // PAR, rows_at + runs + 3, rows_at, rows_at + runs


def make_list(half, int_mask):
    nab, ntile = int_mask.shape
    return pl.pallas_call(
        list_kernel,
        out_shape=jax.ShapeDtypeStruct((list_sizes(nab, ntile)[1],), jnp.int32),
        in_specs=[smem(), smem()],
        out_specs=smem(),
        name="tile_list",
    )(half, int_mask)


def ladder_kernel(nchunk, per, nab, ntile, sides, list_ref, int_ref, *rest):
    chunks, outs, scratch = (
        rest[:nchunk],
        rest[nchunk : nchunk + len(sides)],
        rest[nchunk + len(sides) :],
    )
    dense, bufs, meta_v, meta_s, sems, meta_sem = scratch
    group = RUN * PAR
    _, _, rows_at, steps_at = list_sizes(nab, ntile)
    groups = ntile // GRP
    slots = groups * KEPT
    begin = list_ref[steps_at + sides[0]]
    total = list_ref[steps_at + sides[-1] + 1]

    def start(n):
        slot = lax.rem(n, SLOTS)
        for u in range(group):
            at = list_ref[n * group + u]
            i, t = at // (ntile + 1), lax.rem(at, ntile + 1)
            t = jnp.minimum(t, ntile - 1)
            pltpu.make_async_copy(
                int_ref.at[
                    pl.ds(pl.multiple_of(i * TILE, TILE), TILE),
                    pl.ds(pl.multiple_of(t * TILE, TILE), TILE),
                ],
                bufs.at[slot, u],
                sems.at[slot],
            ).start()

    for n in range(SLOTS):

        @pl.when(begin + n < total)
        def _():
            start(begin + n)

    for c in range(nchunk):
        head = chunks[c][per * slots * PIECE :, :].astype(jnp.float32)
        meta_v[c * 8 : (c + 1) * 8, :] = head[:8].astype(jnp.int32)
    copy = pltpu.make_async_copy(meta_v, meta_s, meta_sem)
    copy.start()
    for out in outs:
        out[...] = jnp.zeros_like(out)
    dense[ntile] = jnp.zeros(dense.shape[1:], jnp.bfloat16)
    copy.wait()
    zero = jnp.zeros((IJ_BLK, LANES), jnp.bfloat16)
    for c in range(nchunk):
        for q in range(per):
            row = (c * per + q) * IJ_BLK
            for g in range(groups):
                bits = meta_s[c * 8, q * groups + g]
                count = jnp.int32(0)
                for j in range(GRP):
                    here = (bits >> j) & 1
                    base = (
                        q * slots + g * KEPT + jnp.minimum(count, KEPT - 1)
                    ) * PIECE
                    for half in range(2):
                        at = pl.multiple_of(base + half * IJ_BLK, IJ_BLK)
                        tile = chunks[c][pl.ds(at, IJ_BLK), :]
                        dense[
                            g * GRP + j,
                            row : row + IJ_BLK,
                            half * LANES : (half + 1) * LANES,
                        ] = jnp.where(here == 1, tile, zero)
                    count += here

    for side, out in zip(sides, outs, strict=True):

        def step(n, carry):
            slot = lax.rem(n, SLOTS)
            pltpu.make_async_copy(bufs.at[slot], bufs.at[slot], sems.at[slot]).wait()
            parts = []
            for r in range(PAR):
                acc = None
                for u in range(r * RUN, (r + 1) * RUN):
                    t = lax.rem(list_ref[n * group + u], ntile + 1)
                    part = lax.dot_general(
                        dense[t],
                        bufs[slot, u],
                        (((1,), (1,)), ((), ())),
                        preferred_element_type=jnp.float32,
                    )
                    acc = part if acc is None else acc + part
                parts.append(acc)
            for r in range(PAR):
                left = pl.multiple_of(list_ref[rows_at + n * PAR + r] * TILE, TILE)
                out[:, pl.ds(left, TILE)] += parts[r]

            @pl.when(n + SLOTS < total)
            def _():
                start(n + SLOTS)

            return carry

        lax.fori_loop(list_ref[steps_at + side], list_ref[steps_at + side + 1], step, 0)


def ladder(chunks, tile_list, integrals, sides):
    nchunk = len(chunks)
    rows_ab, rows_cd = integrals.shape
    ntile = rows_cd // TILE
    per = (chunks[0].shape[0] - META) // (ntile // 2 * PIECE)
    m = nchunk * per * IJ_BLK
    out = jax.ShapeDtypeStruct((m, rows_ab // 2), jnp.float32)
    return pl.pallas_call(
        functools.partial(ladder_kernel, nchunk, per, rows_ab // TILE, ntile, sides),
        out_shape=[out] * len(sides),
        in_specs=[smem(), pl.BlockSpec(memory_space=pl.ANY)]
        + [vmem()] * nchunk,
        out_specs=[vmem()] * len(sides),
        scratch_shapes=[
            VMEM((ntile + 1, m, TILE), jnp.bfloat16),
            VMEM((SLOTS, RUN * PAR, TILE, TILE), jnp.bfloat16),
            VMEM((nchunk * 8, LANES), jnp.int32),
            SMEM((nchunk * 8, LANES), jnp.int32),
            pltpu.SemaphoreType.DMA((SLOTS,)),
            pltpu.SemaphoreType.DMA,
        ],
        compiler_params=pltpu.CompilerParams(vmem_limit_bytes=30 * 2**20),
        cost_estimate=pl.CostEstimate(
            flops=len(sides) * m * rows_ab * rows_cd,
            bytes_accessed=len(sides) * rows_ab * rows_cd // 2,
            transcendentals=0,
        ),
        name="ladder",
    )(tile_list, integrals, *chunks)


def code_kernel(pieces, mine_ref, got_ref, sum_ref, *code_refs):
    width = mine_ref.shape[1]
    above = 0
    for rows, code_ref in zip(pieces, code_refs, strict=True):

        def step(b, carry, above=above, code_ref=code_ref):
            row = pl.multiple_of(b * IJ_BLK, IJ_BLK)
            at, to = pl.ds(above + row, IJ_BLK), pl.ds(row, IJ_BLK)
            total = mine_ref[at, :] + got_ref[at, :]
            sum_ref[at, :] = total
            peak = jnp.max(jnp.abs(total), axis=1, keepdims=True)
            level = jnp.ceil(jnp.log(jnp.maximum(peak, FLOOR)) * (OCTAVE / LN2))
            up = jnp.exp(level * (-LN2 / OCTAVE)) * TOP
            code_ref[to, :width] = (
                jnp.round(total * up).astype(jnp.int32).astype(jnp.int16)
            )
            code_ref[to, width:] = jnp.broadcast_to(
                level.astype(jnp.int32), (IJ_BLK, LANES)
            ).astype(jnp.int16)
            return carry

        lax.fori_loop(0, rows // IJ_BLK, step, 0)
        above += rows


def code(mine, got, pieces):
    rows, width = mine.shape
    return pl.pallas_call(
        functools.partial(code_kernel, pieces),
        out_shape=[jax.ShapeDtypeStruct((rows, width), jnp.float32)]
        + [jax.ShapeDtypeStruct((p, width + LANES), jnp.int16) for p in pieces],
        in_specs=[vmem()] * 2,
        out_specs=[vmem()] * (1 + len(pieces)),
        compiler_params=pltpu.CompilerParams(vmem_limit_bytes=8 * 2**20),
        name="code",
    )(mine, got)


def final_kernel(pieces, npeer, blocks, n, ncol, src_ref, place_ref, occ_ref, vir_ref, *rest):
    out, rest = rest[-1], list(rest)
    sums = [rest.pop(0) for _ in pieces]
    codes = [[[rest.pop(0) for _ in range(npeer)] for _ in cut] for cut in pieces]
    width = vir_ref.shape[1]
    chip, half = place_ref[0], place_ref[1]
    rows_out = out.shape[1]
    vir = vir_ref[...]
    for j, batch in enumerate(blocks):
        for b, (which, block) in enumerate(batch):
            src = src_ref[which]
            owner = src * ncol // n
            row = lax.rem(src, n // ncol) * (rows_out * ncol // n) + block * IJ_BLK
            at = slice(b * IJ_BLK, (b + 1) * IJ_BLK)
            piece, above = 0, 0
            while b * IJ_BLK >= above + pieces[j][piece]:
                above += pieces[j][piece]
                piece += 1
            sent = slice(b * IJ_BLK - above, (b + 1) * IJ_BLK - above)

            @pl.when(owner // 2 == chip)
            def _():
                side = lax.rem(owner + half, 2)
                to = pl.multiple_of(row, IJ_BLK)
                total = sums[j][at, :]
                for got in codes[j][piece]:
                    level = got[sent, width:].astype(jnp.int32).astype(jnp.float32)
                    down = jnp.exp(level[:, :1] * (LN2 / OCTAVE)) * (1.0 / TOP)
                    coded = got[sent, :width].astype(jnp.int32).astype(jnp.float32)
                    total = total + coded * down
                denom = vir - occ_ref[side, pl.ds(to, IJ_BLK), :]
                out[side, pl.ds(to, IJ_BLK), :] = (total / denom).astype(out.dtype)


def final(sums, codes, blocks, n, ncol, src, place, occ, vir, so_far):
    npeer = len(codes[0][0])
    pieces = [[part[0].shape[0] for part in batch] for batch in codes]
    flat = [c for batch in codes for part in batch for c in part]
    width = vir.shape[1]
    more = [] if so_far is None else [so_far]
    return pl.pallas_call(
        functools.partial(final_kernel, pieces, npeer, blocks, n, ncol),
        out_shape=jax.ShapeDtypeStruct((2, occ.shape[1], width), jnp.bfloat16),
        in_specs=[smem(), smem()] + [vmem()] * (2 + len(sums) + len(flat) + len(more)),
        out_specs=vmem(),
        input_output_aliases={4 + len(sums) + len(flat): 0} if more else {},
        compiler_params=pltpu.CompilerParams(vmem_limit_bytes=8 * 2**20),
        name="final",
    )(src, place, occ, vir, *sums, *flat, *more)


def body(n, ncol, amplitudes, amp_mask, integrals, int_mask, occ_energy, vir_energy):
    cycle = list(range(0, n, 2)) + list(range(n - 1, 0, -2))
    ahead = [(cycle[p], cycle[(p + 1) % n]) for p in range(n)]
    behind = [(b, a) for a, b in ahead]
    row, col = lax.axis_index("row"), lax.axis_index("col")
    half = lax.rem(col, 2)
    core = [(c, c ^ 1) for c in range(ncol)]
    nblock = amp_mask.shape[0]
    per = nblock // FLOWS
    table = [None] * n
    for p in range(n):
        table[cycle[p]] = [cycle[p]] + [
            cycle[(p + sign * s) % n] for s in range(1, n) for sign in (-1, 1)
        ]
    src = jnp.array(table, jnp.int32)[row]
    place = jnp.stack([col // 2, half]).astype(jnp.int32)
    width = integrals.shape[0] // 2

    flows = pack(amplitudes, amp_mask)
    tile_list = make_list(half.reshape(1).astype(jnp.int32), int_mask)
    occ_other = lax.ppermute(occ_energy, "col", core)
    occ = jnp.stack([occ_energy, occ_other])[:, :, None]
    vir = lax.dynamic_slice_in_dim(vir_energy, half * width, width)[None, :]

    def tie(arrays, others):
        return lax.optimization_barrier((arrays, others))

    def ladder_of(steps, sides):
        batch = [part for s in steps for part in parts[s]]
        outs = ladder([c for c, _, _ in batch], tile_list, integrals, sides)
        return *outs, [(which, b + q) for _, which, b in batch for q in range(per)]

    def code_of(got, mine, blocks):
        total, *coded = code(mine, got, [mine.shape[0]])
        sent = [
            [
                lax.ppermute(piece, "col", [(c, c ^ (2 * d)) for c in range(ncol)])
                for d in range(1, ncol // 2)
            ]
            for piece in coded
        ]
        return total, sent, blocks

    def after_codes(array, coded):
        if coded:
            total, peers, blocks = coded.pop()
            array, peers = tie(array, peers)
            coded.append((total, peers, blocks))
        return array

    def final_of(coded, so_far):
        sums, codes, blocks = zip(*coded, strict=True)
        return final(sums, codes, blocks, n, ncol, src, place, occ, vir, so_far)

    parts = [[(flows[f], 0, f * per) for f in range(FLOWS)]]
    held = list(flows)
    coded = []
    for s in range(1, n):
        sent = [
            lax.ppermute(h, "row", ahead if f < FLOWS // 2 else behind)
            for f, h in enumerate(held)
        ]
        if s == 1:
            fixed = [tile_list, occ, vir, src, place]
            held, (tile_list, occ, vir, src, place) = tie(sent, fixed)
        elif s == n - 2:
            other, mine, blocks = ladder_of([s - 2, s - 1], (0, 1))
            other = after_codes(other, coded)
            held, (mine, other) = tie(sent, (mine, other))
            got = lax.ppermute(other, "col", core)
        elif s == n - 1:
            coded.append(code_of(got, mine, blocks))
            other, mine, blocks = ladder_of([s - 1], (0, 1))
            other = after_codes(other, coded)
            held, (mine, other) = tie(sent, (mine, other))
            got = lax.ppermute(other, "col", core)
        elif s % 2 == 0:
            other, _ = ladder_of([s - 2, s - 1], (0,))
            other = after_codes(other, coded)
            held, other = tie(sent, other)
            got = lax.ppermute(other, "col", core)
        else:
            mine, blocks = ladder_of([s - 3, s - 2], (1,))
            total, peers, blocks = code_of(got, mine, blocks)
            held, total = tie(sent, total)
            coded.append((total, peers, blocks))
        parts.append(
            [
                (h, 2 * s - 1 + (f >= FLOWS // 2), f * per)
                for f, h in enumerate(held)
            ]
        )
    coded.append(code_of(got, mine, blocks))
    other, mine, blocks = ladder_of([n - 1], (0, 1))
    other = after_codes(other, coded)
    last = code_of(lax.ppermute(other, "col", core), mine, blocks)
    done = final_of([last], final_of(coded, None))
    mine, theirs = done[0], done[1]
    got = lax.ppermute(theirs, "col", core)
    return jnp.where(
        half == 0,
        jnp.concatenate([mine, got], axis=1),
        jnp.concatenate([got, mine], axis=1),
    )


def solution(mesh):
    return jax.shard_map(
        functools.partial(body, mesh.shape["row"], mesh.shape["col"]),
        mesh=mesh,
        in_specs=(
            P("row", "col"),
            P("row", "col"),
            P("row", "col"),
            P("row", "col"),
            P("col"),
            P("row"),
        ),
        out_specs=P("col", "row"),
        check_vma=False,
    )
```

```python
import functools

import jax
import jax.numpy as jnp
from jax import lax
from jax.experimental import pallas as pl
from jax.experimental.pallas import tpu as pltpu
from jax.sharding import PartitionSpec as P

TILE = 256
IJ_BLK = 32
GRP = 8
KEPT = GRP // 2
LANES = 128
META = 16
PIECE = 2 * IJ_BLK
FLOWS = 2
RUN = 3
PAR = 5
SLOTS = 4
TOP = 32000.0
OCTAVE = 64.0
LN2 = 0.6931471805599453
FLOOR = 1e-30
VMEM = pltpu.VMEM
SMEM = pltpu.SMEM


def vmem():
    return pl.BlockSpec(memory_space=VMEM)


def smem():
    return pl.BlockSpec(memory_space=SMEM)


def pack_kernel(mask_ref, amp_ref, *rest):
    outs, (held, sems) = rest[:FLOWS], rest[FLOWS:]
    nblock, ntile = mask_ref.shape
    per = nblock // FLOWS
    groups = ntile // GRP
    slots = groups * KEPT
    lane = lax.broadcasted_iota(jnp.int32, (META, LANES), 1)

    def fetch(block):
        rows = pl.ds(block * IJ_BLK, IJ_BLK)
        return pltpu.make_async_copy(amp_ref.at[rows], held.at[rows], sems.at[block])

    order = [flow * per + q for q in range(per) for flow in range(FLOWS)]
    metas = [jnp.zeros((META, LANES), jnp.int32)] * FLOWS
    for block in order:
        fetch(block).start()
    for block in order:
        flow, q = block // per, block % per
        out = outs[flow]
        rows = slice(block * IJ_BLK, (block + 1) * IJ_BLK)
        fetch(block).wait()
        for g in range(groups):
            count, bits = jnp.int32(0), jnp.int32(0)
            for j in range(GRP):
                t = g * GRP + j
                here = mask_ref[block, t]
                base = (q * slots + g * KEPT + count) * PIECE

                @pl.when(here == 1)
                def _():
                    for half in range(2):
                        at = pl.multiple_of(base + half * IJ_BLK, IJ_BLK)
                        out[pl.ds(at, IJ_BLK), :] = held[
                            rows,
                            t * TILE + half * LANES : t * TILE + (half + 1) * LANES,
                        ]

                count += here
                bits += here << j
            metas[flow] = jnp.where(lane == q * groups + g, bits, metas[flow])
    for flow in range(FLOWS):
        meta = metas[flow].astype(jnp.float32).astype(jnp.bfloat16)
        outs[flow][per * slots * PIECE :, :] = meta


def pack(amplitudes, amp_mask):
    nblock, ntile = amp_mask.shape
    rows = nblock // FLOWS * (ntile // 2) * PIECE + META
    return pl.pallas_call(
        pack_kernel,
        out_shape=[jax.ShapeDtypeStruct((rows, LANES), jnp.bfloat16)] * FLOWS,
        in_specs=[smem(), pl.BlockSpec(memory_space=pl.ANY)],
        out_specs=[vmem()] * FLOWS,
        scratch_shapes=[
            VMEM(amplitudes.shape, jnp.bfloat16),
            pltpu.SemaphoreType.DMA((nblock,)),
        ],
        compiler_params=pltpu.CompilerParams(vmem_limit_bytes=16 * 2**20),
        name="pack",
    )(amp_mask, amplitudes)


def list_kernel(half_ref, mask_ref, list_ref):
    nab, ntile = mask_ref.shape
    steps, size, rows_at, steps_at = list_sizes(nab, ntile)
    first = (1 - half_ref[0]) * (nab // 2)
    none = jnp.int32(ntile)

    def clear(k, carry):
        for u in range(GRP):
            list_ref[k * GRP + u] = none
        return carry

    lax.fori_loop(0, rows_at // GRP, clear, 0)
    for k in range(rows_at, steps_at):
        list_ref[k] = jnp.int32(0)

    def row(ii, base):
        i = lax.rem(ii + first, nab)
        at = base * RUN
        for t in range(ntile):
            here = mask_ref[i, t]
            list_ref[at] = jnp.where(here == 1, i * (ntile + 1) + t, none)
            at += here
        runs = (at - base * RUN + RUN - 1) // RUN

        def note(k, carry):
            list_ref[rows_at + base + k] = lax.rem(ii, nab // 2)
            return carry

        lax.fori_loop(0, runs, note, 0)
        return base + runs

    list_ref[steps_at] = jnp.int32(0)
    middle = lax.fori_loop(0, nab // 2, row, jnp.int32(0))
    middle = (middle + PAR - 1) // PAR
    list_ref[steps_at + 1] = middle
    end = lax.fori_loop(nab // 2, nab, row, middle * PAR)
    list_ref[steps_at + 2] = (end + PAR - 1) // PAR


def list_sizes(nab, ntile):
    runs = nab * ((ntile + RUN - 1) // RUN) + 2 * PAR
    rows_at = -(-(runs * RUN + 1) // GRP) * GRP
    return runs // PAR, rows_at + runs + 3, rows_at, rows_at + runs


def make_list(half, int_mask):
    nab, ntile = int_mask.shape
    return pl.pallas_call(
        list_kernel,
        out_shape=jax.ShapeDtypeStruct((list_sizes(nab, ntile)[1],), jnp.int32),
        in_specs=[smem(), smem()],
        out_specs=smem(),
        name="tile_list",
    )(half, int_mask)


def ladder_kernel(nchunk, per, nab, ntile, sides, list_ref, int_ref, *rest):
    chunks, outs, scratch = (
        rest[:nchunk],
        rest[nchunk : nchunk + len(sides)],
        rest[nchunk + len(sides) :],
    )
    dense, bufs, meta_v, meta_s, sems, meta_sem = scratch
    group = RUN * PAR
    _, _, rows_at, steps_at = list_sizes(nab, ntile)
    groups = ntile // GRP
    slots = groups * KEPT
    begin = list_ref[steps_at + sides[0]]
    total = list_ref[steps_at + sides[-1] + 1]

    def start(n):
        slot = lax.rem(n, SLOTS)
        for u in range(group):
            at = list_ref[n * group + u]
            i, t = at // (ntile + 1), lax.rem(at, ntile + 1)
            t = jnp.minimum(t, ntile - 1)
            pltpu.make_async_copy(
                int_ref.at[
                    pl.ds(pl.multiple_of(i * TILE, TILE), TILE),
                    pl.ds(pl.multiple_of(t * TILE, TILE), TILE),
                ],
                bufs.at[slot, u],
                sems.at[slot],
            ).start()

    for n in range(SLOTS):

        @pl.when(begin + n < total)
        def _():
            start(begin + n)

    for c in range(nchunk):
        head = chunks[c][per * slots * PIECE :, :].astype(jnp.float32)
        meta_v[c * 8 : (c + 1) * 8, :] = head[:8].astype(jnp.int32)
    copy = pltpu.make_async_copy(meta_v, meta_s, meta_sem)
    copy.start()
    for out in outs:
        out[...] = jnp.zeros_like(out)
    dense[ntile] = jnp.zeros(dense.shape[1:], jnp.bfloat16)
    copy.wait()
    zero = jnp.zeros((IJ_BLK, LANES), jnp.bfloat16)
    for c in range(nchunk):
        for q in range(per):
            row = (c * per + q) * IJ_BLK
            for g in range(groups):
                bits = meta_s[c * 8, q * groups + g]
                count = jnp.int32(0)
                for j in range(GRP):
                    here = (bits >> j) & 1
                    base = (
                        q * slots + g * KEPT + jnp.minimum(count, KEPT - 1)
                    ) * PIECE
                    for half in range(2):
                        at = pl.multiple_of(base + half * IJ_BLK, IJ_BLK)
                        tile = chunks[c][pl.ds(at, IJ_BLK), :]
                        dense[
                            g * GRP + j,
                            row : row + IJ_BLK,
                            half * LANES : (half + 1) * LANES,
                        ] = jnp.where(here == 1, tile, zero)
                    count += here

    for side, out in zip(sides, outs, strict=True):

        def step(n, carry):
            slot = lax.rem(n, SLOTS)
            pltpu.make_async_copy(bufs.at[slot], bufs.at[slot], sems.at[slot]).wait()
            parts = []
            for r in range(PAR):
                acc = None
                for u in range(r * RUN, (r + 1) * RUN):
                    t = lax.rem(list_ref[n * group + u], ntile + 1)
                    part = lax.dot_general(
                        dense[t],
                        bufs[slot, u],
                        (((1,), (1,)), ((), ())),
                        preferred_element_type=jnp.float32,
                    )
                    acc = part if acc is None else acc + part
                parts.append(acc)
            for r in range(PAR):
                left = pl.multiple_of(list_ref[rows_at + n * PAR + r] * TILE, TILE)
                out[:, pl.ds(left, TILE)] += parts[r]

            @pl.when(n + SLOTS < total)
            def _():
                start(n + SLOTS)

            return carry

        lax.fori_loop(list_ref[steps_at + side], list_ref[steps_at + side + 1], step, 0)


def ladder(chunks, tile_list, integrals, sides):
    nchunk = len(chunks)
    rows_ab, rows_cd = integrals.shape
    ntile = rows_cd // TILE
    per = (chunks[0].shape[0] - META) // (ntile // 2 * PIECE)
    m = nchunk * per * IJ_BLK
    out = jax.ShapeDtypeStruct((m, rows_ab // 2), jnp.float32)
    return pl.pallas_call(
        functools.partial(ladder_kernel, nchunk, per, rows_ab // TILE, ntile, sides),
        out_shape=[out] * len(sides),
        in_specs=[smem(), pl.BlockSpec(memory_space=pl.ANY)]
        + [vmem()] * nchunk,
        out_specs=[vmem()] * len(sides),
        scratch_shapes=[
            VMEM((ntile + 1, m, TILE), jnp.bfloat16),
            VMEM((SLOTS, RUN * PAR, TILE, TILE), jnp.bfloat16),
            VMEM((nchunk * 8, LANES), jnp.int32),
            SMEM((nchunk * 8, LANES), jnp.int32),
            pltpu.SemaphoreType.DMA((SLOTS,)),
            pltpu.SemaphoreType.DMA,
        ],
        compiler_params=pltpu.CompilerParams(vmem_limit_bytes=30 * 2**20),
        cost_estimate=pl.CostEstimate(
            flops=len(sides) * m * rows_ab * rows_cd,
            bytes_accessed=len(sides) * rows_ab * rows_cd // 2,
            transcendentals=0,
        ),
        name="ladder",
    )(tile_list, integrals, *chunks)


def code_kernel(pieces, mine_ref, got_ref, sum_ref, *code_refs):
    width = mine_ref.shape[1]
    above = 0
    for rows, code_ref in zip(pieces, code_refs, strict=True):

        def step(b, carry, above=above, code_ref=code_ref):
            row = pl.multiple_of(b * IJ_BLK, IJ_BLK)
            at, to = pl.ds(above + row, IJ_BLK), pl.ds(row, IJ_BLK)
            total = mine_ref[at, :] + got_ref[at, :]
            sum_ref[at, :] = total
            peak = jnp.max(jnp.abs(total), axis=1, keepdims=True)
            level = jnp.ceil(jnp.log(jnp.maximum(peak, FLOOR)) * (OCTAVE / LN2))
            up = jnp.exp(level * (-LN2 / OCTAVE)) * TOP
            code_ref[to, :width] = (
                jnp.round(total * up).astype(jnp.int32).astype(jnp.int16)
            )
            code_ref[to, width:] = jnp.broadcast_to(
                level.astype(jnp.int32), (IJ_BLK, LANES)
            ).astype(jnp.int16)
            return carry

        lax.fori_loop(0, rows // IJ_BLK, step, 0)
        above += rows


def code(mine, got, pieces):
    rows, width = mine.shape
    return pl.pallas_call(
        functools.partial(code_kernel, pieces),
        out_shape=[jax.ShapeDtypeStruct((rows, width), jnp.float32)]
        + [jax.ShapeDtypeStruct((p, width + LANES), jnp.int16) for p in pieces],
        in_specs=[vmem()] * 2,
        out_specs=[vmem()] * (1 + len(pieces)),
        compiler_params=pltpu.CompilerParams(vmem_limit_bytes=8 * 2**20),
        name="code",
    )(mine, got)


def final_kernel(pieces, npeer, blocks, n, ncol, src_ref, place_ref, occ_ref, vir_ref, *rest):
    out, rest = rest[-1], list(rest)
    sums = [rest.pop(0) for _ in pieces]
    codes = [[[rest.pop(0) for _ in range(npeer)] for _ in cut] for cut in pieces]
    width = vir_ref.shape[1]
    chip, half = place_ref[0], place_ref[1]
    rows_out = out.shape[1]
    vir = vir_ref[...]
    for j, batch in enumerate(blocks):
        for b, (which, block) in enumerate(batch):
            src = src_ref[which]
            owner = src * ncol // n
            row = lax.rem(src, n // ncol) * (rows_out * ncol // n) + block * IJ_BLK
            at = slice(b * IJ_BLK, (b + 1) * IJ_BLK)
            piece, above = 0, 0
            while b * IJ_BLK >= above + pieces[j][piece]:
                above += pieces[j][piece]
                piece += 1
            sent = slice(b * IJ_BLK - above, (b + 1) * IJ_BLK - above)

            @pl.when(owner // 2 == chip)
            def _():
                side = lax.rem(owner + half, 2)
                to = pl.multiple_of(row, IJ_BLK)
                total = sums[j][at, :]
                for got in codes[j][piece]:
                    level = got[sent, width:].astype(jnp.int32).astype(jnp.float32)
                    down = jnp.exp(level[:, :1] * (LN2 / OCTAVE)) * (1.0 / TOP)
                    coded = got[sent, :width].astype(jnp.int32).astype(jnp.float32)
                    total = total + coded * down
                denom = vir - occ_ref[side, pl.ds(to, IJ_BLK), :]
                out[side, pl.ds(to, IJ_BLK), :] = (total / denom).astype(out.dtype)


def final(sums, codes, blocks, n, ncol, src, place, occ, vir, so_far):
    npeer = len(codes[0][0])
    pieces = [[part[0].shape[0] for part in batch] for batch in codes]
    flat = [c for batch in codes for part in batch for c in part]
    width = vir.shape[1]
    more = [] if so_far is None else [so_far]
    return pl.pallas_call(
        functools.partial(final_kernel, pieces, npeer, blocks, n, ncol),
        out_shape=jax.ShapeDtypeStruct((2, occ.shape[1], width), jnp.bfloat16),
        in_specs=[smem(), smem()] + [vmem()] * (2 + len(sums) + len(flat) + len(more)),
        out_specs=vmem(),
        input_output_aliases={4 + len(sums) + len(flat): 0} if more else {},
        compiler_params=pltpu.CompilerParams(vmem_limit_bytes=8 * 2**20),
        name="final",
    )(src, place, occ, vir, *sums, *flat, *more)


def body(n, ncol, amplitudes, amp_mask, integrals, int_mask, occ_energy, vir_energy):
    cycle = list(range(0, n, 2)) + list(range(n - 1, 0, -2))
    ahead = [(cycle[p], cycle[(p + 1) % n]) for p in range(n)]
    behind = [(b, a) for a, b in ahead]
    row, col = lax.axis_index("row"), lax.axis_index("col")
    half = lax.rem(col, 2)
    core = [(c, c ^ 1) for c in range(ncol)]
    nblock = amp_mask.shape[0]
    per = nblock // FLOWS
    table = [None] * n
    for p in range(n):
        table[cycle[p]] = [cycle[p]] + [
            cycle[(p + sign * s) % n] for s in range(1, n) for sign in (-1, 1)
        ]
    src = jnp.array(table, jnp.int32)[row]
    place = jnp.stack([col // 2, half]).astype(jnp.int32)
    width = integrals.shape[0] // 2

    flows = pack(amplitudes, amp_mask)
    tile_list = make_list(half.reshape(1).astype(jnp.int32), int_mask)
    occ_other = lax.ppermute(occ_energy, "col", core)
    occ = jnp.stack([occ_energy, occ_other])[:, :, None]
    vir = lax.dynamic_slice_in_dim(vir_energy, half * width, width)[None, :]

    def tie(arrays, others):
        return lax.optimization_barrier((arrays, others))

    def ladder_of(steps, sides):
        batch = [part for s in steps for part in parts[s]]
        outs = ladder([c for c, _, _ in batch], tile_list, integrals, sides)
        return *outs, [(which, b + q) for _, which, b in batch for q in range(per)]

    def code_of(got, mine, blocks):
        total, *coded = code(mine, got, [mine.shape[0]])
        sent = [
            [
                lax.ppermute(piece, "col", [(c, c ^ (2 * d)) for c in range(ncol)])
                for d in range(1, ncol // 2)
            ]
            for piece in coded
        ]
        return total, sent, blocks

    def after_codes(array, coded):
        if coded:
            total, peers, blocks = coded.pop()
            array, peers = tie(array, peers)
            coded.append((total, peers, blocks))
        return array

    def final_of(coded, so_far):
        sums, codes, blocks = zip(*coded, strict=True)
        return final(sums, codes, blocks, n, ncol, src, place, occ, vir, so_far)

    parts = [[(flows[f], 0, f * per) for f in range(FLOWS)]]
    held = list(flows)
    coded = []
    for s in range(1, n):
        sent = [
            lax.ppermute(h, "row", ahead if f < FLOWS // 2 else behind)
            for f, h in enumerate(held)
        ]
        if s == 1:
            fixed = [tile_list, occ, vir, src, place]
            held, (tile_list, occ, vir, src, place) = tie(sent, fixed)
        elif s == n - 2:
            other, mine, blocks = ladder_of([s - 2, s - 1], (0, 1))
            other = after_codes(other, coded)
            held, (mine, other) = tie(sent, (mine, other))
            got = lax.ppermute(other, "col", core)
        elif s == n - 1:
            coded.append(code_of(got, mine, blocks))
            other, mine, blocks = ladder_of([s - 1], (0, 1))
            other = after_codes(other, coded)
            held, (mine, other) = tie(sent, (mine, other))
            got = lax.ppermute(other, "col", core)
        elif s % 2 == 0:
            other, _ = ladder_of([s - 2, s - 1], (0,))
            other = after_codes(other, coded)
            held, other = tie(sent, other)
            got = lax.ppermute(other, "col", core)
        else:
            mine, blocks = ladder_of([s - 3, s - 2], (1,))
            total, peers, blocks = code_of(got, mine, blocks)
            held, total = tie(sent, total)
            coded.append((total, peers, blocks))
        parts.append(
            [
                (h, 2 * s - 1 + (f >= FLOWS // 2), f * per)
                for f, h in enumerate(held)
            ]
        )
    coded.append(code_of(got, mine, blocks))
    other, mine, blocks = ladder_of([n - 1], (0, 1))
    other = after_codes(other, coded)
    last = code_of(lax.ppermute(other, "col", core), mine, blocks)
    done = final_of([last], final_of(coded, None))
    mine, theirs = done[0], done[1]
    got = lax.ppermute(theirs, "col", core)
    return jnp.where(
        half == 0,
        jnp.concatenate([mine, got], axis=1),
        jnp.concatenate([got, mine], axis=1),
    )


def solution(mesh):
    return jax.shard_map(
        functools.partial(body, mesh.shape["row"], mesh.shape["col"]),
        mesh=mesh,
        in_specs=(
            P("row", "col"),
            P("row", "col"),
            P("row", "col"),
            P("row", "col"),
            P("col"),
            P("row"),
        ),
        out_specs=P("col", "row"),
        check_vma=False,
    )
```

```python
import functools

import jax
import jax.numpy as jnp
from jax import lax
from jax.experimental import pallas as pl
from jax.experimental.pallas import tpu as pltpu
from jax.sharding import PartitionSpec as P

TILE = 256
IJ_BLK = 32
GRP = 8
KEPT = GRP // 2
LANES = 128
META = 16
PIECE = 2 * IJ_BLK
FLOWS = 2
RUN = 3
PAR = 5
SLOTS = 5
TOP = 32000.0
OCTAVE = 64.0
LN2 = 0.6931471805599453
FLOOR = 1e-30
VMEM = pltpu.VMEM
SMEM = pltpu.SMEM


def vmem():
    return pl.BlockSpec(memory_space=VMEM)


def smem():
    return pl.BlockSpec(memory_space=SMEM)


def pack_kernel(mask_ref, amp_ref, *rest):
    outs, (held, sems) = rest[:FLOWS], rest[FLOWS:]
    nblock, ntile = mask_ref.shape
    per = nblock // FLOWS
    groups = ntile // GRP
    slots = groups * KEPT
    lane = lax.broadcasted_iota(jnp.int32, (META, LANES), 1)

    def fetch(block):
        rows = pl.ds(block * IJ_BLK, IJ_BLK)
        return pltpu.make_async_copy(amp_ref.at[rows], held.at[rows], sems.at[block])

    order = [flow * per + q for q in range(per) for flow in range(FLOWS)]
    metas = [jnp.zeros((META, LANES), jnp.int32)] * FLOWS
    for block in order:
        fetch(block).start()
    for block in order:
        flow, q = block // per, block % per
        out = outs[flow]
        rows = slice(block * IJ_BLK, (block + 1) * IJ_BLK)
        fetch(block).wait()
        for g in range(groups):
            count, bits = jnp.int32(0), jnp.int32(0)
            for j in range(GRP):
                t = g * GRP + j
                here = mask_ref[block, t]
                base = (q * slots + g * KEPT + count) * PIECE

                @pl.when(here == 1)
                def _():
                    for half in range(2):
                        at = pl.multiple_of(base + half * IJ_BLK, IJ_BLK)
                        out[pl.ds(at, IJ_BLK), :] = held[
                            rows,
                            t * TILE + half * LANES : t * TILE + (half + 1) * LANES,
                        ]

                count += here
                bits += here << j
            metas[flow] = jnp.where(lane == q * groups + g, bits, metas[flow])
    for flow in range(FLOWS):
        meta = metas[flow].astype(jnp.float32).astype(jnp.bfloat16)
        outs[flow][per * slots * PIECE :, :] = meta


def pack(amplitudes, amp_mask):
    nblock, ntile = amp_mask.shape
    rows = nblock // FLOWS * (ntile // 2) * PIECE + META
    return pl.pallas_call(
        pack_kernel,
        out_shape=[jax.ShapeDtypeStruct((rows, LANES), jnp.bfloat16)] * FLOWS,
        in_specs=[smem(), pl.BlockSpec(memory_space=pl.ANY)],
        out_specs=[vmem()] * FLOWS,
        scratch_shapes=[
            VMEM(amplitudes.shape, jnp.bfloat16),
            pltpu.SemaphoreType.DMA((nblock,)),
        ],
        compiler_params=pltpu.CompilerParams(vmem_limit_bytes=16 * 2**20),
        name="pack",
    )(amp_mask, amplitudes)


def list_kernel(half_ref, mask_ref, list_ref):
    nab, ntile = mask_ref.shape
    steps, size, rows_at, steps_at = list_sizes(nab, ntile)
    first = (1 - half_ref[0]) * (nab // 2)
    none = jnp.int32(ntile)

    def clear(k, carry):
        for u in range(GRP):
            list_ref[k * GRP + u] = none
        return carry

    lax.fori_loop(0, rows_at // GRP, clear, 0)
    for k in range(rows_at, steps_at):
        list_ref[k] = jnp.int32(0)

    def row(ii, base):
        i = lax.rem(ii + first, nab)
        at = base * RUN
        for t in range(ntile):
            here = mask_ref[i, t]
            list_ref[at] = jnp.where(here == 1, i * (ntile + 1) + t, none)
            at += here
        runs = (at - base * RUN + RUN - 1) // RUN

        def note(k, carry):
            list_ref[rows_at + base + k] = lax.rem(ii, nab // 2)
            return carry

        lax.fori_loop(0, runs, note, 0)
        return base + runs

    list_ref[steps_at] = jnp.int32(0)
    middle = lax.fori_loop(0, nab // 2, row, jnp.int32(0))
    middle = (middle + PAR - 1) // PAR
    list_ref[steps_at + 1] = middle
    end = lax.fori_loop(nab // 2, nab, row, middle * PAR)
    list_ref[steps_at + 2] = (end + PAR - 1) // PAR


def list_sizes(nab, ntile):
    runs = nab * ((ntile + RUN - 1) // RUN) + 2 * PAR
    rows_at = -(-(runs * RUN + 1) // GRP) * GRP
    return runs // PAR, rows_at + runs + 3, rows_at, rows_at + runs


def make_list(half, int_mask):
    nab, ntile = int_mask.shape
    return pl.pallas_call(
        list_kernel,
        out_shape=jax.ShapeDtypeStruct((list_sizes(nab, ntile)[1],), jnp.int32),
        in_specs=[smem(), smem()],
        out_specs=smem(),
        name="tile_list",
    )(half, int_mask)


def ladder_kernel(nchunk, per, nab, ntile, sides, list_ref, int_ref, *rest):
    chunks, outs, scratch = (
        rest[:nchunk],
        rest[nchunk : nchunk + len(sides)],
        rest[nchunk + len(sides) :],
    )
    dense, bufs, meta_v, meta_s, sems, meta_sem = scratch
    group = RUN * PAR
    _, _, rows_at, steps_at = list_sizes(nab, ntile)
    groups = ntile // GRP
    slots = groups * KEPT
    begin = list_ref[steps_at + sides[0]]
    total = list_ref[steps_at + sides[-1] + 1]

    def start(n):
        slot = lax.rem(n, SLOTS)
        for u in range(group):
            at = list_ref[n * group + u]
            i, t = at // (ntile + 1), lax.rem(at, ntile + 1)
            t = jnp.minimum(t, ntile - 1)
            pltpu.make_async_copy(
                int_ref.at[
                    pl.ds(pl.multiple_of(i * TILE, TILE), TILE),
                    pl.ds(pl.multiple_of(t * TILE, TILE), TILE),
                ],
                bufs.at[slot, u],
                sems.at[slot],
            ).start()

    for n in range(SLOTS):

        @pl.when(begin + n < total)
        def _():
            start(begin + n)

    for c in range(nchunk):
        head = chunks[c][per * slots * PIECE :, :].astype(jnp.float32)
        meta_v[c * 8 : (c + 1) * 8, :] = head[:8].astype(jnp.int32)
    copy = pltpu.make_async_copy(meta_v, meta_s, meta_sem)
    copy.start()
    for out in outs:
        out[...] = jnp.zeros_like(out)
    dense[ntile] = jnp.zeros(dense.shape[1:], jnp.bfloat16)
    copy.wait()
    zero = jnp.zeros((IJ_BLK, LANES), jnp.bfloat16)
    for c in range(nchunk):
        for q in range(per):
            row = (c * per + q) * IJ_BLK
            for g in range(groups):
                bits = meta_s[c * 8, q * groups + g]
                count = jnp.int32(0)
                for j in range(GRP):
                    here = (bits >> j) & 1
                    base = (
                        q * slots + g * KEPT + jnp.minimum(count, KEPT - 1)
                    ) * PIECE
                    for half in range(2):
                        at = pl.multiple_of(base + half * IJ_BLK, IJ_BLK)
                        tile = chunks[c][pl.ds(at, IJ_BLK), :]
                        dense[
                            g * GRP + j,
                            row : row + IJ_BLK,
                            half * LANES : (half + 1) * LANES,
                        ] = jnp.where(here == 1, tile, zero)
                    count += here

    for side, out in zip(sides, outs, strict=True):

        def step(n, carry):
            slot = lax.rem(n, SLOTS)
            pltpu.make_async_copy(bufs.at[slot], bufs.at[slot], sems.at[slot]).wait()
            parts = []
            for r in range(PAR):
                acc = None
                for u in range(r * RUN, (r + 1) * RUN):
                    t = lax.rem(list_ref[n * group + u], ntile + 1)
                    part = lax.dot_general(
                        dense[t],
                        bufs[slot, u],
                        (((1,), (1,)), ((), ())),
                        preferred_element_type=jnp.float32,
                    )
                    acc = part if acc is None else acc + part
                parts.append(acc)
            for r in range(PAR):
                left = pl.multiple_of(list_ref[rows_at + n * PAR + r] * TILE, TILE)
                out[:, pl.ds(left, TILE)] += parts[r]

            @pl.when(n + SLOTS < total)
            def _():
                start(n + SLOTS)

            return carry

        lax.fori_loop(list_ref[steps_at + side], list_ref[steps_at + side + 1], step, 0)


def ladder(chunks, tile_list, integrals, sides):
    nchunk = len(chunks)
    rows_ab, rows_cd = integrals.shape
    ntile = rows_cd // TILE
    per = (chunks[0].shape[0] - META) // (ntile // 2 * PIECE)
    m = nchunk * per * IJ_BLK
    out = jax.ShapeDtypeStruct((m, rows_ab // 2), jnp.float32)
    return pl.pallas_call(
        functools.partial(ladder_kernel, nchunk, per, rows_ab // TILE, ntile, sides),
        out_shape=[out] * len(sides),
        in_specs=[smem(), pl.BlockSpec(memory_space=pl.ANY)]
        + [vmem()] * nchunk,
        out_specs=[vmem()] * len(sides),
        scratch_shapes=[
            VMEM((ntile + 1, m, TILE), jnp.bfloat16),
            VMEM((SLOTS, RUN * PAR, TILE, TILE), jnp.bfloat16),
            VMEM((nchunk * 8, LANES), jnp.int32),
            SMEM((nchunk * 8, LANES), jnp.int32),
            pltpu.SemaphoreType.DMA((SLOTS,)),
            pltpu.SemaphoreType.DMA,
        ],
        compiler_params=pltpu.CompilerParams(vmem_limit_bytes=30 * 2**20),
        cost_estimate=pl.CostEstimate(
            flops=len(sides) * m * rows_ab * rows_cd,
            bytes_accessed=len(sides) * rows_ab * rows_cd // 2,
            transcendentals=0,
        ),
        name="ladder",
    )(tile_list, integrals, *chunks)


def code_kernel(pieces, mine_ref, got_ref, sum_ref, *code_refs):
    width = mine_ref.shape[1]
    above = 0
    for rows, code_ref in zip(pieces, code_refs, strict=True):

        def step(b, carry, above=above, code_ref=code_ref):
            row = pl.multiple_of(b * IJ_BLK, IJ_BLK)
            at, to = pl.ds(above + row, IJ_BLK), pl.ds(row, IJ_BLK)
            total = mine_ref[at, :] + got_ref[at, :]
            sum_ref[at, :] = total
            peak = jnp.max(jnp.abs(total), axis=1, keepdims=True)
            level = jnp.ceil(jnp.log(jnp.maximum(peak, FLOOR)) * (OCTAVE / LN2))
            up = jnp.exp(level * (-LN2 / OCTAVE)) * TOP
            code_ref[to, :width] = (
                jnp.round(total * up).astype(jnp.int32).astype(jnp.int16)
            )
            code_ref[to, width:] = jnp.broadcast_to(
                level.astype(jnp.int32), (IJ_BLK, LANES)
            ).astype(jnp.int16)
            return carry

        lax.fori_loop(0, rows // IJ_BLK, step, 0)
        above += rows


def code(mine, got, pieces):
    rows, width = mine.shape
    return pl.pallas_call(
        functools.partial(code_kernel, pieces),
        out_shape=[jax.ShapeDtypeStruct((rows, width), jnp.float32)]
        + [jax.ShapeDtypeStruct((p, width + LANES), jnp.int16) for p in pieces],
        in_specs=[vmem()] * 2,
        out_specs=[vmem()] * (1 + len(pieces)),
        compiler_params=pltpu.CompilerParams(vmem_limit_bytes=8 * 2**20),
        name="code",
    )(mine, got)


def final_kernel(pieces, npeer, blocks, n, ncol, src_ref, place_ref, occ_ref, vir_ref, *rest):
    out, rest = rest[-1], list(rest)
    sums = [rest.pop(0) for _ in pieces]
    codes = [[[rest.pop(0) for _ in range(npeer)] for _ in cut] for cut in pieces]
    width = vir_ref.shape[1]
    chip, half = place_ref[0], place_ref[1]
    rows_out = out.shape[1]
    vir = vir_ref[...]
    for j, batch in enumerate(blocks):
        for b, (which, block) in enumerate(batch):
            src = src_ref[which]
            owner = src * ncol // n
            row = lax.rem(src, n // ncol) * (rows_out * ncol // n) + block * IJ_BLK
            at = slice(b * IJ_BLK, (b + 1) * IJ_BLK)
            piece, above = 0, 0
            while b * IJ_BLK >= above + pieces[j][piece]:
                above += pieces[j][piece]
                piece += 1
            sent = slice(b * IJ_BLK - above, (b + 1) * IJ_BLK - above)

            @pl.when(owner // 2 == chip)
            def _():
                side = lax.rem(owner + half, 2)
                to = pl.multiple_of(row, IJ_BLK)
                total = sums[j][at, :]
                for got in codes[j][piece]:
                    level = got[sent, width:].astype(jnp.int32).astype(jnp.float32)
                    down = jnp.exp(level[:, :1] * (LN2 / OCTAVE)) * (1.0 / TOP)
                    coded = got[sent, :width].astype(jnp.int32).astype(jnp.float32)
                    total = total + coded * down
                denom = vir - occ_ref[side, pl.ds(to, IJ_BLK), :]
                out[side, pl.ds(to, IJ_BLK), :] = (total / denom).astype(out.dtype)


def final(sums, codes, blocks, n, ncol, src, place, occ, vir, so_far):
    npeer = len(codes[0][0])
    pieces = [[part[0].shape[0] for part in batch] for batch in codes]
    flat = [c for batch in codes for part in batch for c in part]
    width = vir.shape[1]
    more = [] if so_far is None else [so_far]
    return pl.pallas_call(
        functools.partial(final_kernel, pieces, npeer, blocks, n, ncol),
        out_shape=jax.ShapeDtypeStruct((2, occ.shape[1], width), jnp.bfloat16),
        in_specs=[smem(), smem()] + [vmem()] * (2 + len(sums) + len(flat) + len(more)),
        out_specs=vmem(),
        input_output_aliases={4 + len(sums) + len(flat): 0} if more else {},
        compiler_params=pltpu.CompilerParams(vmem_limit_bytes=8 * 2**20),
        name="final",
    )(src, place, occ, vir, *sums, *flat, *more)


def body(n, ncol, amplitudes, amp_mask, integrals, int_mask, occ_energy, vir_energy):
    cycle = list(range(0, n, 2)) + list(range(n - 1, 0, -2))
    ahead = [(cycle[p], cycle[(p + 1) % n]) for p in range(n)]
    behind = [(b, a) for a, b in ahead]
    row, col = lax.axis_index("row"), lax.axis_index("col")
    half = lax.rem(col, 2)
    core = [(c, c ^ 1) for c in range(ncol)]
    nblock = amp_mask.shape[0]
    per = nblock // FLOWS
    table = [None] * n
    for p in range(n):
        table[cycle[p]] = [cycle[p]] + [
            cycle[(p + sign * s) % n] for s in range(1, n) for sign in (-1, 1)
        ]
    src = jnp.array(table, jnp.int32)[row]
    place = jnp.stack([col // 2, half]).astype(jnp.int32)
    width = integrals.shape[0] // 2

    flows = pack(amplitudes, amp_mask)
    tile_list = make_list(half.reshape(1).astype(jnp.int32), int_mask)
    occ_other = lax.ppermute(occ_energy, "col", core)
    occ = jnp.stack([occ_energy, occ_other])[:, :, None]
    vir = lax.dynamic_slice_in_dim(vir_energy, half * width, width)[None, :]

    def tie(arrays, others):
        return lax.optimization_barrier((arrays, others))

    def ladder_of(steps, sides):
        batch = [part for s in steps for part in parts[s]]
        outs = ladder([c for c, _, _ in batch], tile_list, integrals, sides)
        return *outs, [(which, b + q) for _, which, b in batch for q in range(per)]

    def code_of(got, mine, blocks):
        total, *coded = code(mine, got, [mine.shape[0]])
        sent = [
            [
                lax.ppermute(piece, "col", [(c, c ^ (2 * d)) for c in range(ncol)])
                for d in range(1, ncol // 2)
            ]
            for piece in coded
        ]
        return total, sent, blocks

    def after_codes(array, coded):
        if coded:
            total, peers, blocks = coded.pop()
            array, peers = tie(array, peers)
            coded.append((total, peers, blocks))
        return array

    def final_of(coded, so_far):
        sums, codes, blocks = zip(*coded, strict=True)
        return final(sums, codes, blocks, n, ncol, src, place, occ, vir, so_far)

    parts = [[(flows[f], 0, f * per) for f in range(FLOWS)]]
    held = list(flows)
    coded = []
    for s in range(1, n):
        sent = [
            lax.ppermute(h, "row", ahead if f < FLOWS // 2 else behind)
            for f, h in enumerate(held)
        ]
        if s == 1:
            fixed = [tile_list, occ, vir, src, place]
            held, (tile_list, occ, vir, src, place) = tie(sent, fixed)
        elif s == n - 2:
            other, mine, blocks = ladder_of([s - 2, s - 1], (0, 1))
            other = after_codes(other, coded)
            held, (mine, other) = tie(sent, (mine, other))
            got = lax.ppermute(other, "col", core)
        elif s == n - 1:
            coded.append(code_of(got, mine, blocks))
            other, mine, blocks = ladder_of([s - 1], (0, 1))
            other = after_codes(other, coded)
            held, (mine, other) = tie(sent, (mine, other))
            got = lax.ppermute(other, "col", core)
        elif s % 2 == 0:
            other, _ = ladder_of([s - 2, s - 1], (0,))
            other = after_codes(other, coded)
            held, other = tie(sent, other)
            got = lax.ppermute(other, "col", core)
        else:
            mine, blocks = ladder_of([s - 3, s - 2], (1,))
            total, peers, blocks = code_of(got, mine, blocks)
            held, total = tie(sent, total)
            coded.append((total, peers, blocks))
        parts.append(
            [
                (h, 2 * s - 1 + (f >= FLOWS // 2), f * per)
                for f, h in enumerate(held)
            ]
        )
    coded.append(code_of(got, mine, blocks))
    other, mine, blocks = ladder_of([n - 1], (0, 1))
    other = after_codes(other, coded)
    last = code_of(lax.ppermute(other, "col", core), mine, blocks)
    done = final_of([last], final_of(coded, None))
    mine, theirs = done[0], done[1]
    got = lax.ppermute(theirs, "col", core)
    return jnp.where(
        half == 0,
        jnp.concatenate([mine, got], axis=1),
        jnp.concatenate([got, mine], axis=1),
    )


def solution(mesh):
    return jax.shard_map(
        functools.partial(body, mesh.shape["row"], mesh.shape["col"]),
        mesh=mesh,
        in_specs=(
            P("row", "col"),
            P("row", "col"),
            P("row", "col"),
            P("row", "col"),
            P("col"),
            P("row"),
        ),
        out_specs=P("col", "row"),
        check_vma=False,
    )
```
